32 devices in a mesh: group: 4 (over y, x), member: 8 (over z, core).
Axes of the slice: x: 2, y: 2, z: 4, core: 2. Of those that a mesh axis runs over, the one named last changes fastest.
Arguments:
- entity: bfloat16 [8192, 800], P(('group', 'member')), may hold values from -3 to 7.5
- adagrad_state: float32 [8192], P(('group', 'member')), may hold values from 0.01 to 1
- relation: bfloat16 [1345, 800], replicated, may hold values from -1.8 to 1.8
- source_ids: int32 [2, 16384], P(None, ('group', 'member')), may hold values from 0 to 255
- relation_ids: int32 [2, 16384], P(None, ('group', 'member')), may hold values from 0 to 1344
- dest_groups: int32 [2, 16384, 1], P(None, ('group', 'member')), may hold values from 0 to 3; in each aligned block of 512 rows (0 to 511, 512 to 1023, ..., all dimensions but the last counted through in order) at most 256 rows name the same one
- dest_rows: int32 [2, 16384], P(None, ('group', 'member')), may hold values from 0 to 255
- negative_ids: int32 [2, 32000], P(None, ('group', 'member')), may hold values from 0 to 255
- owners: int32 [2, 4], replicated, may hold values from 0 to 7
Outputs:
- new_entity: bfloat16 [8192, 800], P(('group', 'member'))
- new_state: float32 [8192], P(('group', 'member'))
The draws below stay inside these ranges and needn't reach their ends.
Inputs may be any that keep to these rules, and one draw needn't show every extreme that they name: `dest_groups`: for each sub-step and each device's 512 edges, at most 256 name any one destination group, a bound that some block reaches.
All inputs are finite; a program needn't handle non-finite values.
Results may differ from the reference program's by a relative error of at most 0.017.
Values may be sent and summed in bfloat16 or wider, within the bound.
No kernel may reach another device: no remote copies, remote signals or barrier semaphores. Data moves between devices by JAX's collectives and lax.ppermute only.
A program may use at most 64 MiB of HBM per device.

```python
import math
import jax
import jax.numpy as jnp
import numpy as np
from jax import lax

DIM = 400
REL = 1345
NEG = 1000
SUBSTEPS = 2
ROWS_DEV = 256
EDGES = 512
CAP = 256
ENTITIES = 8192
EDGES_ALL = 16384
NEG_ALL = 32000
N_GROUP = 4
N_MEMBER = 8


def draw_entity(key, part):
    first = jax.random.fold_in(key, 0)
    values = jnp.clip(jax.random.normal(first, (ENTITIES, 2 * DIM), jnp.float32), -6.0, 6.0)
    out = values * 0.5
    return out.astype(jnp.bfloat16)


def draw_relation(key, part):
    first = jax.random.fold_in(key, 0)
    values = jnp.clip(jax.random.normal(first, (REL, 2 * DIM), jnp.float32), -6.0, 6.0)
    out = values * 0.3
    return out.astype(jnp.bfloat16)


def place_ends(array, rng, low, high):
    index_at = [jax.random.randint(jax.random.fold_in(rng, axis), (), 0, length) for axis, length in enumerate(array.shape)]
    widest = array.shape.index(max(array.shape))
    beside = index_at[:widest] + [(index_at[widest] + 1) % array.shape[widest]] + index_at[widest + 1:]
    return array.at[tuple(index_at)].set(low).at[tuple(beside)].set(high)


def levels(key, shape, shards, smallest, largest):
    loudness, own = 1.0, jax.random.fold_in(key, 6)
    for dim, parts in shards:
        draws = jnp.exp(jax.random.uniform(jax.random.fold_in(own, dim), (parts,), jnp.float32, smallest / len(shards), largest / len(shards)))
        loudness = loudness * jnp.repeat(draws, shape[dim] // parts).reshape([-1 if axis == dim else 1 for axis in range(len(shape))])
    return loudness


def cumulative_ranks(number_of, slope):
    loads = [(1 << 20) // math.isqrt(grade ** slope) + 1 for grade in range(1, number_of + 1)]
    spread = 1 + sum(loads) // (1 << 30)
    return np.cumsum(np.array([max(1, weight // spread) for weight in loads]))


def skewed_ids(stream_key, extent, number_of, lean):
    table = cumulative_ranks(number_of, lean)
    lot = jax.random.randint(jax.random.fold_in(stream_key, 1), extent, 0, int(table[number_of - 1]))
    standing = jnp.searchsorted(jnp.asarray(table, jnp.int32), lot, side="right")
    return jax.random.permutation(jax.random.fold_in(stream_key, 2), number_of)[standing].astype(jnp.int32)


def routed_block(rng, own, number, rows, number_of, top, most, lean):
    order = jax.random.permutation(rng, number_of)
    heavy_load, usual = portions_of(number_of, rows * top, most, lean, True), portions_of(number_of, rows * top, most, lean, False)
    places = jnp.arange(number_of)

    def named(tallies, turn):
        used = int((tallies > 0).sum())
        fixed = max(1, used // 4)
        moved = fixed + (places - fixed + turn * (used - fixed)) % max(1, number_of - fixed)
        return jnp.zeros((number_of,), jnp.int32).at[order[jnp.where(places < fixed, places, moved)]].set(jnp.asarray(tallies, jnp.int32))

    tallies = jnp.where(number % 4 == 0, named(heavy_load, number // 4), named(usual, number - number // 4 - 1))
    mixed = jax.random.permutation(jax.random.fold_in(own, 3), number_of)
    donor, sink = mixed[0:number_of // 2 * 2:2], mixed[1:number_of // 2 * 2:2]
    slack = jnp.minimum(tallies[donor] - 1, most - tallies[sink]) // 2
    slack = jnp.where((donor == order[0]) | (sink == order[0]) | (tallies[sink] == 0), 0, jnp.maximum(slack, 0))
    moved = jax.random.randint(jax.random.fold_in(own, 4), (number_of // 2,), 0, 1 << 20) % (slack + 1)
    tallies = tallies.at[donor].add(-moved).at[sink].add(moved)
    items = jnp.searchsorted(jnp.cumsum(tallies), jnp.arange(rows * top), side="right").astype(jnp.int32)
    grid = items.reshape(top, rows).T
    grid = grid[jax.random.permutation(jax.random.fold_in(own, 1), rows)]
    turn = jax.random.randint(jax.random.fold_in(own, 2), (rows, 1), 0, top)
    return jnp.take_along_axis(grid, (jnp.arange(top)[None, :] + turn) % top, axis=1)


def portions_of(number_of, total, bound, lean, full):
    loads = [(1 << 20) // math.isqrt(grade ** lean) + 1 for grade in range(1, number_of + 1)]
    largest = bound if full else min(bound, max(-(-total // number_of), total * loads[0] // sum(loads)))
    least = 1 if total - largest >= number_of - 1 else 0
    given, spare = [largest] + [least] * (number_of - 1), total - largest - least * (number_of - 1)
    while spare > 0:
        free = [i for i in range(1, number_of) if given[i] < largest] or [i for i in range(1, number_of) if given[i] < bound]
        whole, remaining = sum([loads[i] for i in free]), spare
        for i in free:
            extra = min(bound - given[i], max(1, remaining * loads[i] // whole), spare)
            given[i] = given[i] + extra
            spare = spare - extra
    return np.array(given)


def setup_inputs(seed: int = 0) -> dict:
    arg_keys = jax.random.split(jax.random.key(seed), 10)
    entity = draw_entity(jax.random.fold_in(arg_keys[9], 71), 0)
    adagrad_state = jnp.clip(jnp.exp(math.log(1.0) - 4.6051702 * jax.random.uniform(arg_keys[1], (ENTITIES,), jnp.float32) ** levels(arg_keys[1], (ENTITIES,), ((0, 32),), -0.2, 0.2)), 0.01, 1.0)
    relation = draw_relation(jax.random.fold_in(arg_keys[9], 71), 0)
    source_ids = place_ends(jax.random.randint(arg_keys[3], (SUBSTEPS, EDGES_ALL), 0, ROWS_DEV), jax.random.fold_in(arg_keys[3], 1), 0, ROWS_DEV - 1).astype(jnp.int32)
    relation_ids = place_ends(skewed_ids(arg_keys[4], (SUBSTEPS, EDGES_ALL), REL, 2), jax.random.fold_in(arg_keys[4], 3), 0, REL - 1).astype(jnp.int32)
    dest_groups_keys = jax.random.split(jax.random.fold_in(arg_keys[5], 1), SUBSTEPS * EDGES_ALL // EDGES)
    dest_groups_turns = jax.random.permutation(jax.random.fold_in(arg_keys[5], 3), SUBSTEPS * EDGES_ALL // EDGES)
    dest_groups = jax.vmap(lambda own, number: routed_block(jax.random.fold_in(arg_keys[5], 2), own, number, EDGES, N_GROUP, 1, CAP, 2))(dest_groups_keys, dest_groups_turns).reshape((SUBSTEPS, EDGES_ALL, 1))
    dest_rows = place_ends(jax.random.randint(arg_keys[6], (SUBSTEPS, EDGES_ALL), 0, ROWS_DEV), jax.random.fold_in(arg_keys[6], 1), 0, ROWS_DEV - 1).astype(jnp.int32)
    negative_ids = place_ends(jax.random.randint(arg_keys[7], (SUBSTEPS, NEG_ALL), 0, ROWS_DEV), jax.random.fold_in(arg_keys[7], 1), 0, ROWS_DEV - 1).astype(jnp.int32)
    owners = place_ends(jax.random.randint(arg_keys[8], (SUBSTEPS, N_GROUP), 0, N_MEMBER), jax.random.fold_in(arg_keys[8], 1), 0, N_MEMBER - 1).astype(jnp.int32)
    return dict(entity=entity, adagrad_state=adagrad_state, relation=relation, source_ids=source_ids, relation_ids=relation_ids, dest_groups=dest_groups, dest_rows=dest_rows, negative_ids=negative_ids, owners=owners)


def complex_query(source, rel):
    half = source.shape[-1] // 2
    sr, si = (source[..., :half], source[..., half:])
    rr, ri = (rel[..., :half], rel[..., half:])
    return jnp.concatenate([sr * rr - si * ri, sr * ri + si * rr], -1)

def source_grad(grad_query, rel):
    half = grad_query.shape[-1] // 2
    gr, gi = (grad_query[..., :half], grad_query[..., half:])
    rr, ri = (rel[..., :half], rel[..., half:])
    return jnp.concatenate([gr * rr + gi * ri, gi * rr - gr * ri], -1)

def edge_terms(source_rows, rel_rows, dest_rows, negatives):
    rel = rel_rows.astype(jnp.float32)
    query = complex_query(source_rows.astype(jnp.float32), rel).astype(jnp.bfloat16)
    dest = dest_rows.astype(jnp.float32)
    positive = lax.optimization_barrier(jnp.sum(query.astype(jnp.float32) * dest, -1))
    scores = lax.dot_general(query, negatives, (((1,), (1,)), ((), ())), preferred_element_type=jnp.float32)
    top = jnp.maximum(lax.optimization_barrier(jnp.max(scores, 1)), positive)
    pos_exp = jnp.exp(positive - top)
    neg_exp = jnp.exp(scores - top[:, None])
    total = pos_exp + lax.optimization_barrier(jnp.sum(neg_exp, 1))
    coef_pos = pos_exp / total - 1.0
    coef_neg = (neg_exp / total[:, None]).astype(jnp.bfloat16)
    grad_query = coef_pos[:, None] * dest + jnp.dot(coef_neg, negatives, preferred_element_type=jnp.float32)
    grad_source = source_grad(grad_query, rel)
    grad_dest = coef_pos[:, None] * query.astype(jnp.float32)
    grad_neg = lax.dot_general(coef_neg, query, (((0,), (0,)), ((), ())), preferred_element_type=jnp.float32)
    return (grad_source, grad_dest, grad_neg)

def reference(entity, adagrad_state, relation, source_ids, relation_ids, dest_groups, dest_rows, negative_ids, owners):
    members = N_MEMBER
    count = N_GROUP * N_MEMBER
    width = entity.shape[1]
    table = entity.reshape(count, ROWS_DEV, width)
    state = adagrad_state.reshape(count, ROWS_DEV)
    for step in range(SUBSTEPS):
        src = source_ids[step].reshape(count, EDGES)
        rel = relation_ids[step].reshape(count, EDGES)
        dgr = dest_groups[step, :, 0].reshape(count, EDGES)
        drw = dest_rows[step].reshape(count, EDGES)
        neg = negative_ids[step].reshape(count, NEG)
        own = owners[step]

        def visit(total, device):
            grp = device // members
            mem = device % members
            owner_dev = (grp * members + own[grp]).astype(jnp.int32)
            block = table[owner_dev]
            dest_dev = (dgr[device] * members + mem).astype(jnp.int32)
            source_rows = block[src[device]]
            rel_rows = relation[rel[device]]
            dest_vals = table[dest_dev, drw[device]]
            negatives = table[device][neg[device]]
            grad_source, grad_dest, grad_neg = edge_terms(source_rows, rel_rows, dest_vals, negatives)
            total = total.at[owner_dev, src[device]].add(grad_source)
            total = total.at[dest_dev, drw[device]].add(grad_dest)
            total = total.at[device, neg[device]].add(grad_neg)
            return (total, None)
        grads, _ = lax.scan(visit, jnp.zeros((count, ROWS_DEV, width), jnp.float32), jnp.arange(count, dtype=jnp.int32))
        state = state + lax.optimization_barrier(jnp.mean(grads * grads, -1))
        table = (table.astype(jnp.float32) - 1.0 * grads / jnp.sqrt(state)[..., None]).astype(jnp.bfloat16)
    return (table.reshape(count * ROWS_DEV, width), state.reshape(count * ROWS_DEV))
```

```python
import functools

import jax
import jax.numpy as jnp
from jax import lax
from jax.experimental import pallas as pl
from jax.experimental.pallas import tpu as pltpu
from jax.sharding import PartitionSpec as P

BF = jnp.bfloat16
F32 = jnp.float32
LANES = 128
VMEM = pl.BlockSpec(memory_space=pltpu.VMEM)
SMEM = pl.BlockSpec(memory_space=pltpu.SMEM)
PARAMS = pltpu.CompilerParams(vmem_limit_bytes=14 * 1024 * 1024)


def call(body, outs, *args, smem=()):
    return pl.pallas_call(
        body,
        out_shape=outs,
        in_specs=[SMEM if i in smem else VMEM for i in range(len(args))],
        out_specs=[VMEM] * len(outs),
        compiler_params=PARAMS,
        cost_estimate=pl.CostEstimate(flops=1000, bytes_accessed=1000, transcendentals=0),
    )(*args)


def sds(shape, dtype):
    return jax.ShapeDtypeStruct(shape, dtype)


def onehot(row, count, base=0):
    sub = lax.broadcasted_iota(jnp.int32, (count, row.shape[1]), 0) + base
    return (sub == row).astype(F32).astype(BF)


def dot(a, b):
    return jnp.dot(a, b, preferred_element_type=F32)


def dot_t(a, b):
    return lax.dot_general(a, b, (((1,), (1,)), ((), ())), preferred_element_type=F32)


def dot_c(a, b):
    return lax.dot_general(a, b, (((0,), (0,)), ((), ())), preferred_element_type=F32)


def masks_body(owners, *outs):
    group, member = lax.axis_index("group"), lax.axis_index("member")
    per_step = len(outs) // owners.shape[0]
    for step in range(owners.shape[0]):
        root = owners[step, group]
        differ = root ^ member
        for index in range(per_step - 1):
            bit = (differ >> index) & 1
            outs[step * per_step + index][...] = jnp.full(outs[0].shape, bit, jnp.int32)
        outs[(step + 1) * per_step - 1][...] = jnp.full(outs[0].shape, (root == member).astype(jnp.int32))


def prepare_body(step, rel_ids, neg_ids, relation, tail, rel, counts):
    full = relation.shape[1] // LANES * LANES
    hot = onehot(rel_ids[step : step + 1, :], full + LANES)
    rel[...] = (dot(relation[:, :full], hot[:full]) + dot(tail[...], hot[full:])).astype(BF)
    negs = neg_ids[step : step + 1, :]
    sub = lax.broadcasted_iota(jnp.int32, (counts.shape[0], negs.shape[1]), 0)
    counts[...] = jnp.sum((sub == negs).astype(F32), 1, keepdims=True)


def query_body(step, src, real, imag, rel, table, counts, query, probs, top, total):
    rows, half = table.shape[1], real.shape[0]
    hot = onehot(src[step : step + 1, :], rows)
    sr, si = dot(real[...], hot), dot(imag[...], hot)
    rr, ri = rel[:half, :].astype(F32), rel[half:, :].astype(F32)
    query[:half, :] = (sr * rr - si * ri).astype(BF)
    query[half:, :] = (sr * ri + si * rr).astype(BF)
    scores = dot_c(table[...], query[...])
    count = counts[...]
    scores = jnp.where(count > 0.0, scores, -jnp.inf)
    best = jnp.max(scores, 0, keepdims=True)
    prob = count * jnp.exp(scores - best)
    probs[...] = prob
    top[...] = best
    total[...] = jnp.sum(prob, 0, keepdims=True)


def place(step, groups, count, rows, dest_groups, dest_rows, first=0):
    near = dest_groups[step] ^ lax.axis_index("group")
    return onehot(near * rows + dest_rows[step : step + 1, :], count * rows, first * rows)


def dest_body(step, groups, dest_groups, dest_rows, table, *refs):
    shards, dest = refs[:-1], refs[-1]
    hot = place(step, groups, groups - 1, table.shape[1], dest_groups, dest_rows)
    whole = jnp.concatenate([x[...] for x in (table, *shards)], 1)
    dest[...] = dot(whole, hot).astype(BF)


def source_body(
    step, groups, src, dest_groups, dest_rows, query, probs, top_neg, total_neg, rel, table, dest, far_r, far_i,
    out_r, out_i, coef_pos, coef_neg,
):
    rows, half = table.shape[1], out_r.shape[0]
    hot = place(step, groups, 1, rows, dest_groups, dest_rows, groups - 1)
    dr = dest[:half, :].astype(F32) + dot(far_r[...], hot)
    di = dest[half:, :].astype(F32) + dot(far_i[...], hot)
    qr, qi = query[:half, :].astype(F32), query[half:, :].astype(F32)
    positive = jnp.sum(qr * dr + qi * di, 0, keepdims=True)
    best = top_neg[...]
    top = jnp.maximum(best, positive)
    pos_exp = jnp.exp(positive - top)
    scale = jnp.exp(best - top)
    total = pos_exp + scale * total_neg[...]
    pos = pos_exp / total - 1.0
    neg = (probs[...] * (scale / total)).astype(BF)
    coef_pos[...] = pos
    coef_neg[...] = neg
    gr = pos * dr + dot(table[:half, :], neg)
    gi = pos * di + dot(table[half:, :], neg)
    rr, ri = rel[:half, :].astype(F32), rel[half:, :].astype(F32)
    back = onehot(src[step : step + 1, :], rows)
    out_r[...] = dot_t((gr * rr + gi * ri).astype(BF), back).astype(BF)
    out_i[...] = dot_t((gi * rr - gr * ri).astype(BF), back).astype(BF)


def spread_body(step, groups, dest_groups, dest_rows, query, coef_pos, coef_neg, base_grad, *sends):
    rows, half = base_grad.shape[1], base_grad.shape[0] // 2
    hot = place(step, groups, groups, rows, dest_groups, dest_rows)
    for part in (0, 1):
        span = slice(part * half, (part + 1) * half)
        q = query[span, :]
        spread = dot_t((coef_pos[...] * q.astype(F32)).astype(BF), hot)
        base_grad[span, :] = spread[:, :rows] + dot_t(q, coef_neg[...])
        grads = [spread[:, k * rows : (k + 1) * rows].astype(BF) for k in range(1, groups)]
        if groups == 4:
            sends[part][:half, :] = grads[2]
            sends[part][half:, :] = grads[part]
            sends[2 + part][...] = grads[1 - part]
        else:
            for send, grad in zip(sends, grads):
                send[span, :] = grad


def update_body(halves, table, state, base_grad, src_r, src_i, *refs):
    parts = refs[: len(halves)]
    new_table, new_state = refs[len(halves) :]
    width, half = table.shape[0], src_r.shape[0]
    grads = []
    for part, source in enumerate((src_r, src_i)):
        span = slice(part * half, (part + 1) * half)
        grad = base_grad[span, :] + source[...].astype(F32)
        for piece, held in zip(parts, halves):
            if held is None:
                grad = grad + piece[span, :].astype(F32)
            elif held == part:
                grad = grad + piece[...].astype(F32)
        grads.append(grad)
    square = sum(jnp.sum(g * g, 0, keepdims=True) for g in grads)
    after = state[...] + square * (1.0 / width)
    new_state[...] = after
    rate = lax.rsqrt(after)
    for part, grad in enumerate(grads):
        span = slice(part * half, (part + 1) * half)
        new_table[span, :] = (table[span, :].astype(F32) - grad * rate).astype(BF)


def add(a, b):
    return (a.astype(F32) + b.astype(F32)).astype(BF)


def shift(value, axis, bit):
    size = lax.axis_size(axis)
    return lax.ppermute(value, axis, [(i, i ^ bit) for i in range(size)])


def z_bits():
    bits = []
    bit = 2
    while bit < lax.axis_size("member"):
        bits.append(bit)
        bit *= 2
    return bits[::-1]


def after(value, *others):
    return lax.optimization_barrier((value, *others))[0]


def cut(value):
    at = (value.shape[0] // 2 + 15) // 16 * 16
    return [value[:at], value[at:]]


def gather_shards(table):
    groups, half = lax.axis_size("group"), table.shape[0] // 2
    near = [shift(table, "group", k) for k in range(1, groups - 1)]
    if groups != 4:
        far = [shift(table[:half], "group", groups - 1), shift(table[half:], "group", groups - 1)]
    else:
        far = [shift(near[0][:half], "group", 2), shift(near[1][half:], "group", 1)]
    return near + far


def spread_grads(sends):
    groups, half = lax.axis_size("group"), sends[0].shape[0] // 2
    if groups != 4:
        got = [shift(x, "group", k + 1) for k, x in enumerate(sends)]
        return got[:2], [(None, x) for x in got]
    x, y = shift(sends[0], "group", 1), shift(sends[1], "group", 2)
    y_real = shift(add(sends[2], x[:half]), "group", 2)
    x_imag = shift(add(sends[3], y[:half]), "group", 1)
    return [x, y], [(0, y_real), (1, x_imag), (0, x[half:]), (1, y[half:])]


def per_device(
    entity,
    adagrad_state,
    relation,
    source_ids,
    relation_ids,
    dest_groups,
    dest_rows,
    negative_ids,
    owners,
):
    groups = lax.axis_size("group")
    first = lax.axis_index("member") % 2 == 0
    steps, edges = source_ids.shape
    rows, width = entity.shape
    half = width // 2
    table = entity.T
    state = adagrad_state[None, :]
    rel_t = relation.T
    full = rel_t.shape[1] // LANES * LANES
    groups = lax.axis_size("group")
    dest_groups = jnp.transpose(dest_groups, (0, 2, 1))
    bits = z_bits()
    kinds = 2 + len(bits)

    def root_masks(owners):
        return call(masks_body, [sds((1, rows), jnp.int32)] * (steps * kinds), owners, smem=(0,))

    def prepare(step, earlier):
        held = after(rel_t, earlier)
        tail = jnp.pad(held[:, full:], ((0, 0), (0, LANES - rel_t.shape[1] + full)))
        return call(
            functools.partial(prepare_body, step),
            [sds((width, edges), BF), sds((rows, 1), F32)],
            relation_ids, negative_ids, held, tail,
        )

    for step in range(steps):
        real, imag = table[:half], table[half:]
        keep, give = jnp.where(first, real, imag), jnp.where(first, imag, real)
        if step == 0:
            keep, give = lax.optimization_barrier((keep, give))
            masks = root_masks(after(owners, give))
        mask = [x != 0 for x in masks[step * kinds : (step + 1) * kinds]]
        shards = gather_shards(table)
        held = jnp.where(mask[0], shift(give, "member", 1), keep)
        (dest,) = call(
            functools.partial(dest_body, step, groups),
            [sds((width, edges), BF)],
            dest_groups, dest_rows, table, *shards[:-2],
        )
        pieces = cut(held)
        for turn in range(len(bits)):
            if turn == 1:
                pieces[1] = after(pieces[1], *shards[:-2])
            for index, bit in enumerate((bits[turn], bits[-1 - turn])):
                got = shift(pieces[index], "member", bit)
                pieces[index] = jnp.where(mask[bit.bit_length() - 1], got, pieces[index])
        pieces[1] = after(pieces[1], shards[-1], dest)
        others = [shift(x, "member", 1) for x in pieces]
        block = [jnp.concatenate([jnp.where(first, x, y) for x, y in zip(*pair)], 0) for pair in ((pieces, others), (others, pieces))]
        if step == 0:
            rel, counts = prepare(0, pieces[0])
        query, probs, top, total = call(
            functools.partial(query_body, step),
            [sds((width, edges), BF), sds((rows, edges), F32), sds((1, edges), F32), sds((1, edges), F32)],
            source_ids, *block, rel, table, counts,
        )
        out_r, out_i, coef_pos, coef_neg = call(
            functools.partial(source_body, step, groups),
            [sds((half, rows), BF)] * 2 + [sds((1, edges), F32), sds((rows, edges), BF)],
            source_ids, dest_groups, dest_rows, query, probs, top, total, rel, table, dest, *shards[-2:],
        )
        give = shift(jnp.where(first, out_i, out_r), "member", 1)
        shapes = [(width, rows)] * 2 + [(half, rows)] * 2 if groups == 4 else [(width, rows)] * (groups - 1)
        base_grad, *sends = call(
            functools.partial(spread_body, step, groups),
            [sds((width, rows), F32)] + [sds(shape, BF) for shape in shapes],
            dest_groups, dest_rows, query, coef_pos, coef_neg,
        )
        early, parts = spread_grads(sends)
        part = add(jnp.where(first, out_r, out_i), give)
        pieces = cut(part)
        for turn in range(len(bits)):
            for index, bit in enumerate((bits[turn], bits[-1 - turn])):
                pieces[index] = add(pieces[index], shift(pieces[index], "member", bit))
            if turn == 0:
                if step + 1 < steps:
                    ahead = prepare(step + 1, pieces[0])
                    state = after(state, *ahead)
                pieces[1] = after(pieces[1], *early)
        pieces[1] = after(pieces[1], parts[0][1])
        others = [shift(x, "member", 1) for x in pieces]
        source = []
        for pair in ((pieces, others), (others, pieces)):
            both = jnp.concatenate([jnp.where(first, x, y) for x, y in zip(*pair)], 0)
            source.append(jnp.where(mask[-1], both, 0))
        table, state = call(
            functools.partial(update_body, [at for at, _ in parts]),
            [sds((width, rows), BF), sds((1, rows), F32)],
            table, state, base_grad, *source, *[p for _, p in parts],
        )
        if step + 1 < steps:
            rel, counts = ahead
    return (table.T, state[0])


def solution(mesh):
    placed = (
        P(("group", "member"), None),
        P(("group", "member")),
        P(),
        P(None, ("group", "member")),
        P(None, ("group", "member")),
        P(None, ("group", "member"), None),
        P(None, ("group", "member")),
        P(None, ("group", "member")),
        P(),
    )
    return jax.shard_map(
        per_device,
        mesh=mesh,
        in_specs=placed,
        out_specs=(P(("group", "member"), None), P(("group", "member"))),
        check_vma=False,
    )
```

```python
import functools

import jax
import jax.numpy as jnp
from jax import lax
from jax.experimental import pallas as pl
from jax.experimental.pallas import tpu as pltpu
from jax.sharding import PartitionSpec as P

BF = jnp.bfloat16
F32 = jnp.float32
LANES = 128
VMEM = pl.BlockSpec(memory_space=pltpu.VMEM)
SMEM = pl.BlockSpec(memory_space=pltpu.SMEM)
PARAMS = pltpu.CompilerParams(vmem_limit_bytes=14 * 1024 * 1024)


def call(body, outs, *args, smem=(), flops=1000):
    return pl.pallas_call(
        body,
        out_shape=outs,
        in_specs=[SMEM if i in smem else VMEM for i in range(len(args))],
        out_specs=[VMEM] * len(outs),
        compiler_params=PARAMS,
        cost_estimate=pl.CostEstimate(flops=flops, bytes_accessed=1000, transcendentals=0),
    )(*args)


def sds(shape, dtype):
    return jax.ShapeDtypeStruct(shape, dtype)


def onehot(row, count, base=0):
    sub = lax.broadcasted_iota(jnp.int32, (count, row.shape[1]), 0) + base
    return (sub == row).astype(F32).astype(BF)


def dot(a, b):
    return jnp.dot(a, b, preferred_element_type=F32)


def dot_t(a, b):
    return lax.dot_general(a, b, (((1,), (1,)), ((), ())), preferred_element_type=F32)


def dot_c(a, b):
    return lax.dot_general(a, b, (((0,), (0,)), ((), ())), preferred_element_type=F32)


def masks_body(owners, *outs):
    group, member = lax.axis_index("group"), lax.axis_index("member")
    per_step = len(outs) // owners.shape[0]
    for step in range(owners.shape[0]):
        root = owners[step, group]
        differ = root ^ member
        for index in range(per_step - 1):
            bit = (differ >> index) & 1
            outs[step * per_step + index][...] = jnp.full(outs[0].shape, bit, jnp.int32)
        outs[(step + 1) * per_step - 1][...] = jnp.full(outs[0].shape, (root == member).astype(jnp.int32))


def prepare_body(step, rel_ids, neg_ids, relation, tail, rel, counts):
    full = relation.shape[1] // LANES * LANES
    hot = onehot(rel_ids[step : step + 1, :], full + LANES)
    rel[...] = (dot(relation[:, :full], hot[:full]) + dot(tail[...], hot[full:])).astype(BF)
    negs = neg_ids[step : step + 1, :]
    sub = lax.broadcasted_iota(jnp.int32, (counts.shape[0], negs.shape[1]), 0)
    counts[...] = jnp.sum((sub == negs).astype(F32), 1, keepdims=True)


def query_body(step, src, real, imag, rel, table, counts, query, probs, top, total):
    rows, half = table.shape[1], real.shape[0]
    hot = onehot(src[step : step + 1, :], rows)
    sr, si = dot(real[...], hot), dot(imag[...], hot)
    rr, ri = rel[:half, :].astype(F32), rel[half:, :].astype(F32)
    query[:half, :] = (sr * rr - si * ri).astype(BF)
    query[half:, :] = (sr * ri + si * rr).astype(BF)
    scores = dot_c(table[...], query[...])
    count = counts[...]
    scores = jnp.where(count > 0.0, scores, -jnp.inf)
    best = jnp.max(scores, 0, keepdims=True)
    prob = count * jnp.exp(scores - best)
    probs[...] = prob
    top[...] = best
    total[...] = jnp.sum(prob, 0, keepdims=True)


def place(step, groups, count, rows, dest_groups, dest_rows, first=0):
    near = dest_groups[step] ^ lax.axis_index("group")
    return onehot(near * rows + dest_rows[step : step + 1, :], count * rows, first * rows)


def dest_body(step, groups, dest_groups, dest_rows, table, *refs):
    shards, dest = refs[:-1], refs[-1]
    hot = place(step, groups, groups - 1, table.shape[1], dest_groups, dest_rows)
    whole = jnp.concatenate([x[...] for x in (table, *shards)], 1)
    dest[...] = dot(whole, hot).astype(BF)


def far_body(step, groups, dest_groups, dest_rows, near, far_r, far_i, dest):
    rows, half = far_r.shape[1], far_r.shape[0]
    hot = place(step, groups, 1, rows, dest_groups, dest_rows, groups - 1)
    for part, far in enumerate((far_r, far_i)):
        span = slice(part * half, (part + 1) * half)
        dest[span, :] = near[span, :] + dot(far[...], hot).astype(BF)


def source_body(
    step, src, query, probs, top_neg, total_neg, rel, table, dest, out_r, out_i, coef_pos, coef_neg
):
    rows, half = table.shape[1], out_r.shape[0]
    dr, di = dest[:half, :].astype(F32), dest[half:, :].astype(F32)
    qr, qi = query[:half, :].astype(F32), query[half:, :].astype(F32)
    positive = jnp.sum(qr * dr + qi * di, 0, keepdims=True)
    best = top_neg[...]
    top = jnp.maximum(best, positive)
    pos_exp = jnp.exp(positive - top)
    scale = jnp.exp(best - top)
    total = pos_exp + scale * total_neg[...]
    pos = pos_exp / total - 1.0
    neg = (probs[...] * (scale / total)).astype(BF)
    coef_pos[...] = pos
    coef_neg[...] = neg
    gr = pos * dr + dot(table[:half, :], neg)
    gi = pos * di + dot(table[half:, :], neg)
    rr, ri = rel[:half, :].astype(F32), rel[half:, :].astype(F32)
    back = onehot(src[step : step + 1, :], rows)
    out_r[...] = dot_t((gr * rr + gi * ri).astype(BF), back).astype(BF)
    out_i[...] = dot_t((gi * rr - gr * ri).astype(BF), back).astype(BF)


def spread_body(step, groups, dest_groups, dest_rows, query, coef_pos, coef_neg, base_grad, *sends):
    rows, half = base_grad.shape[1], base_grad.shape[0] // 2
    hot = place(step, groups, groups, rows, dest_groups, dest_rows)
    for part in (0, 1):
        span = slice(part * half, (part + 1) * half)
        q = query[span, :]
        spread = dot_t((coef_pos[...] * q.astype(F32)).astype(BF), hot)
        base_grad[span, :] = spread[:, :rows] + dot_t(q, coef_neg[...])
        grads = [spread[:, k * rows : (k + 1) * rows].astype(BF) for k in range(1, groups)]
        if groups == 4:
            sends[part][:half, :] = grads[2]
            sends[part][half:, :] = grads[part]
            sends[2 + part][...] = grads[1 - part]
        else:
            for send, grad in zip(sends, grads):
                send[span, :] = grad


def merge_body(halves, base_grad, *refs):
    half = base_grad.shape[0] // 2
    for part in (0, 1):
        span = slice(part * half, (part + 1) * half)
        grad = base_grad[span, :]
        for piece, held in zip(refs[:-1], halves):
            if held is None:
                grad = grad + piece[span, :].astype(F32)
            elif held == part:
                grad = grad + piece[...].astype(F32)
        refs[-1][span, :] = grad


def update_body(table, state, merged, src_r, src_i, new_table, new_state):
    width, half = table.shape[0], src_r.shape[0]
    grads = []
    for part, source in enumerate((src_r, src_i)):
        grads.append(merged[part * half : (part + 1) * half, :] + source[...].astype(F32))
    square = sum(jnp.sum(g * g, 0, keepdims=True) for g in grads)
    after = state[...] + square * (1.0 / width)
    new_state[...] = after
    rate = lax.rsqrt(after)
    for part, grad in enumerate(grads):
        span = slice(part * half, (part + 1) * half)
        new_table[span, :] = (table[span, :].astype(F32) - grad * rate).astype(BF)


def add(a, b):
    return (a.astype(F32) + b.astype(F32)).astype(BF)


def shift(value, axis, bit):
    size = lax.axis_size(axis)
    return lax.ppermute(value, axis, [(i, i ^ bit) for i in range(size)])


def z_bits():
    bits = []
    bit = 2
    while bit < lax.axis_size("member"):
        bits.append(bit)
        bit *= 2
    return bits


def after(value, *others):
    return lax.optimization_barrier((value, *others))[0]


def gather_shards(table):
    groups, half = lax.axis_size("group"), table.shape[0] // 2
    near = [shift(table, "group", k) for k in range(1, groups - 1)]
    if groups != 4:
        far = [shift(table[:half], "group", groups - 1), shift(table[half:], "group", groups - 1)]
    else:
        far = [shift(near[0][:half], "group", 2), shift(near[1][half:], "group", 1)]
    return near + far


def spread_grads(sends):
    groups, half = lax.axis_size("group"), sends[0].shape[0] // 2
    if groups != 4:
        got = [(None, shift(x, "group", k + 1)) for k, x in enumerate(sends)]
        return lambda *earlier: got
    x, y = shift(sends[0], "group", 1), shift(sends[1], "group", 2)

    def rest(*earlier):
        y_real = shift(add(after(sends[2], *earlier), x[:half]), "group", 2)
        x_imag = shift(add(after(sends[3], *earlier), y[:half]), "group", 1)
        return [(0, y_real), (1, x_imag), (0, x[half:]), (1, y[half:])]

    return rest


def per_device(
    entity,
    adagrad_state,
    relation,
    source_ids,
    relation_ids,
    dest_groups,
    dest_rows,
    negative_ids,
    owners,
):
    groups = lax.axis_size("group")
    first = lax.axis_index("member") % 2 == 0
    steps, edges = source_ids.shape
    rows, width = entity.shape
    half = width // 2
    table = entity.T
    state = adagrad_state[None, :]
    rel_t = relation.T
    full = rel_t.shape[1] // LANES * LANES
    groups = lax.axis_size("group")
    dest_groups = jnp.transpose(dest_groups, (0, 2, 1))
    bits = z_bits()
    kinds = 2 + len(bits)

    def root_masks(owners):
        return call(masks_body, [sds((1, rows), jnp.int32)] * (steps * kinds), owners, smem=(0,))

    def prepare(step, earlier):
        held = after(rel_t, earlier)
        tail = jnp.pad(held[:, full:], ((0, 0), (0, LANES - rel_t.shape[1] + full)))
        return call(
            functools.partial(prepare_body, step),
            [sds((width, edges), BF), sds((rows, 1), F32)],
            relation_ids, negative_ids, held, tail,
        )

    for step in range(steps):
        real, imag = table[:half], table[half:]
        keep, give = jnp.where(first, real, imag), jnp.where(first, imag, real)
        if step == 0:
            keep, give = lax.optimization_barrier((keep, give))
            masks = root_masks(after(owners, give))
        mask = [x != 0 for x in masks[step * kinds : (step + 1) * kinds]]
        shards = gather_shards(table)
        held = jnp.where(mask[0], shift(give, "member", 1), keep)
        for turn, bit in enumerate(bits):
            held = jnp.where(mask[bit.bit_length() - 1], shift(held, "member", bit), held)
        (near,) = call(
            functools.partial(dest_body, step, groups),
            [sds((width, edges), BF)],
            dest_groups, dest_rows, table, *shards[:-2],
        )
        other = shift(after(held, near), "member", 1)
        block = jnp.where(first, held, other), jnp.where(first, other, held)
        if step == 0:
            rel, counts = prepare(0, shards[0])
        (dest,) = call(
            functools.partial(far_body, step, groups),
            [sds((width, edges), BF)],
            dest_groups, dest_rows, near, *shards[-2:],
            flops=8 * 10**9,
        )
        query, probs, top, total = call(
            functools.partial(query_body, step),
            [sds((width, edges), BF), sds((rows, edges), F32), sds((1, edges), F32), sds((1, edges), F32)],
            after(source_ids, dest), *block, rel, table, counts,
        )
        out_r, out_i, coef_pos, coef_neg = call(
            functools.partial(source_body, step),
            [sds((half, rows), BF)] * 2 + [sds((1, edges), F32), sds((rows, edges), BF)],
            source_ids, query, probs, top, total, rel, table, dest,
        )
        give = shift(jnp.where(first, out_i, out_r), "member", 1)
        shapes = [(width, rows)] * 2 + [(half, rows)] * 2 if groups == 4 else [(width, rows)] * (groups - 1)
        base_grad, *sends = call(
            functools.partial(spread_body, step, groups),
            [sds((width, rows), F32)] + [sds(shape, BF) for shape in shapes],
            dest_groups, dest_rows, query, coef_pos, coef_neg,
        )
        rest = spread_grads(sends)
        part = add(jnp.where(first, out_r, out_i), after(give, base_grad))
        for turn, bit in enumerate(bits):
            part = add(part, shift(part, "member", bit))
            if turn == 0:
                parts = rest(part)
                if step + 1 < steps:
                    ahead = prepare(step + 1, part)
        if step + 1 < steps:
            part = after(part, *ahead)
        other = shift(part, "member", 1)
        source = [jnp.where(mask[-1] & first, part, jnp.where(mask[-1], other, 0))]
        source += [jnp.where(mask[-1] & first, other, jnp.where(mask[-1], part, 0))]
        (merged,) = call(
            functools.partial(merge_body, [at for at, _ in parts]),
            [sds((width, rows), F32)],
            base_grad, *[x for _, x in parts],
            flops=8 * 10**9,
        )
        table, state = call(
            update_body, [sds((width, rows), BF), sds((1, rows), F32)], table, state, merged, *source
        )
        if step + 1 < steps:
            rel, counts = ahead
    return (table.T, state[0])


def solution(mesh):
    placed = (
        P(("group", "member"), None),
        P(("group", "member")),
        P(),
        P(None, ("group", "member")),
        P(None, ("group", "member")),
        P(None, ("group", "member"), None),
        P(None, ("group", "member")),
        P(None, ("group", "member")),
        P(),
    )
    return jax.shard_map(
        per_device,
        mesh=mesh,
        in_specs=placed,
        out_specs=(P(("group", "member"), None), P(("group", "member"))),
        check_vma=False,
    )
```

```python
import functools

import jax
import jax.numpy as jnp
from jax import lax
from jax.experimental import pallas as pl
from jax.experimental.pallas import tpu as pltpu
from jax.sharding import PartitionSpec as P

BF = jnp.bfloat16
F32 = jnp.float32
LANES = 128
VMEM = pl.BlockSpec(memory_space=pltpu.VMEM)
SMEM = pl.BlockSpec(memory_space=pltpu.SMEM)
PARAMS = pltpu.CompilerParams(vmem_limit_bytes=14 * 1024 * 1024)


def call(body, outs, *args, smem=(), flops=1000):
    return pl.pallas_call(
        body,
        out_shape=outs,
        in_specs=[SMEM if i in smem else VMEM for i in range(len(args))],
        out_specs=[VMEM] * len(outs),
        compiler_params=PARAMS,
        cost_estimate=pl.CostEstimate(flops=flops, bytes_accessed=1000, transcendentals=0),
    )(*args)


def sds(shape, dtype):
    return jax.ShapeDtypeStruct(shape, dtype)


def onehot(row, count, base=0):
    sub = lax.broadcasted_iota(jnp.int32, (count, row.shape[1]), 0) + base
    return (sub == row).astype(F32).astype(BF)


def dot(a, b):
    return jnp.dot(a, b, preferred_element_type=F32)


def dot_t(a, b):
    return lax.dot_general(a, b, (((1,), (1,)), ((), ())), preferred_element_type=F32)


def dot_c(a, b):
    return lax.dot_general(a, b, (((0,), (0,)), ((), ())), preferred_element_type=F32)


def masks_body(owners, *outs):
    group, member = lax.axis_index("group"), lax.axis_index("member")
    per_step = len(outs) // owners.shape[0]
    for step in range(owners.shape[0]):
        root = owners[step, group]
        differ = root ^ member
        for index in range(per_step - 1):
            bit = (differ >> index) & 1
            outs[step * per_step + index][...] = jnp.full(outs[0].shape, bit, jnp.int32)
        outs[(step + 1) * per_step - 1][...] = jnp.full(outs[0].shape, (root == member).astype(jnp.int32))


def prepare_body(step, rel_ids, neg_ids, relation, rel, counts):
    hot = onehot(rel_ids[step : step + 1, :], relation.shape[1])
    rel[...] = dot(relation[...], hot).astype(BF)
    negs = neg_ids[step : step + 1, :]
    sub = lax.broadcasted_iota(jnp.int32, (counts.shape[0], negs.shape[1]), 0)
    counts[...] = jnp.sum((sub == negs).astype(F32), 1, keepdims=True)


def place(step, groups, count, rows, dest_groups, dest_rows, first=0):
    near = dest_groups[step] ^ lax.axis_index("group")
    return onehot(near * rows + dest_rows[step : step + 1, :], count * rows, first * rows)


def dest_body(step, groups, dest_groups, dest_rows, table, *refs):
    shards, dest = refs[:-1], refs[-1]
    hot = place(step, groups, groups - 1, table.shape[1], dest_groups, dest_rows)
    whole = jnp.concatenate([x[...] for x in (table, *shards)], 1)
    dest[...] = dot(whole, hot).astype(BF)


def far_body(step, groups, dest_groups, dest_rows, near, first, second, dest):
    rows, at = first.shape[1], first.shape[0]
    hot = place(step, groups, 1, rows, dest_groups, dest_rows, groups - 1)
    dest[:at, :] = near[:at, :] + dot(first[...], hot).astype(BF)
    dest[at:, :] = near[at:, :] + dot(second[...], hot).astype(BF)


def source_body(
    step, src, real, imag, rel, table, counts, dest, query, out_r, out_i, coef_pos, coef_neg
):
    rows, half = table.shape[1], real.shape[0]
    back = onehot(src[step : step + 1, :], rows)
    sr, si = dot(real[...], back), dot(imag[...], back)
    rr, ri = rel[:half, :].astype(F32), rel[half:, :].astype(F32)
    query[:half, :] = (sr * rr - si * ri).astype(BF)
    query[half:, :] = (sr * ri + si * rr).astype(BF)
    scores = dot_c(table[...], query[...])
    count = counts[...]
    scores = jnp.where(count > 0.0, scores, -jnp.inf)
    dr, di = dest[:half, :].astype(F32), dest[half:, :].astype(F32)
    qr, qi = query[:half, :].astype(F32), query[half:, :].astype(F32)
    positive = jnp.sum(qr * dr + qi * di, 0, keepdims=True)
    top = jnp.maximum(jnp.max(scores, 0, keepdims=True), positive)
    pos_exp = jnp.exp(positive - top)
    neg_exp = count * jnp.exp(scores - top)
    total = pos_exp + jnp.sum(neg_exp, 0, keepdims=True)
    pos = pos_exp / total - 1.0
    neg = (neg_exp * (1.0 / total)).astype(BF)
    coef_pos[...] = pos
    coef_neg[...] = neg
    gr = pos * dr + dot(table[:half, :], neg)
    gi = pos * di + dot(table[half:, :], neg)
    out_r[...] = dot_t((gr * rr + gi * ri).astype(BF), back).astype(BF)
    out_i[...] = dot_t((gi * rr - gr * ri).astype(BF), back).astype(BF)


def spread_body(step, groups, dest_groups, dest_rows, query, coef_pos, coef_neg, base_grad, *sends):
    rows, half = base_grad.shape[1], base_grad.shape[0] // 2
    hot = place(step, groups, groups, rows, dest_groups, dest_rows)
    for part in (0, 1):
        span = slice(part * half, (part + 1) * half)
        q = query[span, :]
        spread = dot_t((coef_pos[...] * q.astype(F32)).astype(BF), hot)
        base_grad[span, :] = spread[:, :rows] + dot_t(q, coef_neg[...])
        for k in range(1, groups):
            sends[2 * k - 2 + part][...] = spread[:, k * rows : (k + 1) * rows].astype(BF)


def merge_body(halves, base_grad, *refs):
    half = base_grad.shape[0] // 2
    for part in (0, 1):
        span = slice(part * half, (part + 1) * half)
        grad = base_grad[span, :]
        for piece, held in zip(refs[:-1], halves):
            if held is None:
                grad = grad + piece[span, :].astype(F32)
            elif held == part:
                grad = grad + piece[...].astype(F32)
        refs[-1][span, :] = grad


def update_body(table, state, merged, src_r, src_i, new_table, new_state):
    width, half = table.shape[0], src_r.shape[0]
    grads = []
    for part, source in enumerate((src_r, src_i)):
        grads.append(merged[part * half : (part + 1) * half, :] + source[...].astype(F32))
    square = sum(jnp.sum(g * g, 0, keepdims=True) for g in grads)
    after = state[...] + square * (1.0 / width)
    new_state[...] = after
    rate = lax.rsqrt(after)
    for part, grad in enumerate(grads):
        span = slice(part * half, (part + 1) * half)
        new_table[span, :] = (table[span, :].astype(F32) - grad * rate).astype(BF)


def add(a, b):
    return (a.astype(F32) + b.astype(F32)).astype(BF)


def shift(value, axis, bit):
    size = lax.axis_size(axis)
    return lax.ppermute(value, axis, [(i, i ^ bit) for i in range(size)])


def z_bits():
    bits = []
    bit = 2
    while bit < lax.axis_size("member"):
        bits.append(bit)
        bit *= 2
    return bits


def after(value, *others):
    return lax.optimization_barrier((value, *others))[0]


def gather_shards(table):
    groups, width = lax.axis_size("group"), table.shape[0]
    near = [shift(table, "group", k) for k in range(1, groups - 1)]
    if groups != 4:
        far = shift(table, "group", groups - 1)
        return near + [far[: width // 2], far[width // 2 :]]
    at = width * 3 // 5 // 16 * 16
    return near + [shift(near[0][:at], "group", 2), shift(near[1][at:], "group", 1)]


def spread_grads(sends):
    groups = lax.axis_size("group")
    if groups != 4:
        parts = [(p, shift(sends[2 * k - 2 + p], "group", k)) for k in range(1, groups) for p in (0, 1)]
        return [x for _, x in parts[:2]], lambda *earlier: parts
    xr, xi, yr, yi, dr, di = sends
    x, y = shift(dr, "group", 1), shift(di, "group", 2)
    real, imag = shift(xr, "group", 1), shift(yi, "group", 2)

    def rest(*earlier):
        y_real = shift(add(after(yr, *earlier), x), "group", 2)
        x_imag = shift(add(after(xi, *earlier), y), "group", 1)
        return [(0, y_real), (1, x_imag), (0, real), (1, imag)]

    return [x, y], rest


def per_device(
    entity,
    adagrad_state,
    relation,
    source_ids,
    relation_ids,
    dest_groups,
    dest_rows,
    negative_ids,
    owners,
):
    groups = lax.axis_size("group")
    first = lax.axis_index("member") % 2 == 0
    steps, edges = source_ids.shape
    rows, width = entity.shape
    half = width // 2
    table = entity.T
    state = adagrad_state[None, :]
    rel_t = relation.T
    dest_groups = jnp.transpose(dest_groups, (0, 2, 1))
    bits = z_bits()
    kinds = 2 + len(bits)

    def root_masks(owners):
        return call(masks_body, [sds((1, rows), jnp.int32)] * (steps * kinds), owners, smem=(0,))

    def prepare(step, earlier):
        return call(
            functools.partial(prepare_body, step),
            [sds((width, edges), BF), sds((rows, 1), F32)],
            relation_ids, negative_ids, after(rel_t, earlier),
        )

    for step in range(steps):
        real, imag = table[:half], table[half:]
        keep, give = jnp.where(first, real, imag), jnp.where(first, imag, real)
        if step == 0:
            keep, give = lax.optimization_barrier((keep, give))
            masks = root_masks(after(owners, give))
        mask = [x != 0 for x in masks[step * kinds : (step + 1) * kinds]]
        shards = gather_shards(table)
        held = jnp.where(mask[0], shift(give, "member", 1), keep)
        for turn, bit in enumerate(bits):
            held = jnp.where(mask[bit.bit_length() - 1], shift(held, "member", bit), held)
        (near,) = call(
            functools.partial(dest_body, step, groups),
            [sds((width, edges), BF)],
            dest_groups, dest_rows, table, *shards[:-2],
        )
        other = shift(after(held, near), "member", 1)
        block = jnp.where(first, held, other), jnp.where(first, other, held)
        if step == 0:
            rel, counts = prepare(0, shards[0])
        (dest,) = call(
            functools.partial(far_body, step, groups),
            [sds((width, edges), BF)],
            dest_groups, dest_rows, near, *shards[-2:],
            flops=8 * 10**9,
        )
        query, out_r, out_i, coef_pos, coef_neg = call(
            functools.partial(source_body, step),
            [sds((width, edges), BF)]
            + [sds((half, rows), BF)] * 2
            + [sds((1, edges), F32), sds((rows, edges), BF)],
            source_ids, *block, rel, table, counts, dest,
        )
        give = shift(jnp.where(first, out_i, out_r), "member", 1)
        base_grad, *sends = call(
            functools.partial(spread_body, step, groups),
            [sds((width, rows), F32)] + [sds((half, rows), BF)] * (2 * groups - 2),
            dest_groups, dest_rows, query, coef_pos, coef_neg,
        )
        early, rest = spread_grads(sends)
        part = add(jnp.where(first, out_r, out_i), after(give, base_grad))
        for turn, bit in enumerate(bits):
            part = add(part, shift(part, "member", bit))
            if turn == 0:
                parts = rest(part)
                if step + 1 < steps:
                    ahead = prepare(step + 1, part)
        if step + 1 < steps:
            part = after(part, *ahead)
        other = shift(part, "member", 1)
        source = [jnp.where(mask[-1] & first, part, jnp.where(mask[-1], other, 0))]
        source += [jnp.where(mask[-1] & first, other, jnp.where(mask[-1], part, 0))]
        (merged,) = call(
            functools.partial(merge_body, [at for at, _ in parts]),
            [sds((width, rows), F32)],
            base_grad, *[x for _, x in parts],
            flops=8 * 10**9,
        )
        table, state = call(
            update_body, [sds((width, rows), BF), sds((1, rows), F32)], table, state, merged, *source
        )
        if step + 1 < steps:
            rel, counts = ahead
    return (table.T, state[0])


def solution(mesh):
    placed = (
        P(("group", "member"), None),
        P(("group", "member")),
        P(),
        P(None, ("group", "member")),
        P(None, ("group", "member")),
        P(None, ("group", "member"), None),
        P(None, ("group", "member")),
        P(None, ("group", "member")),
        P(),
    )
    return jax.shard_map(
        per_device,
        mesh=mesh,
        in_specs=placed,
        out_specs=(P(("group", "member"), None), P(("group", "member"))),
        check_vma=False,
    )
```

```python
import functools

import jax
import jax.numpy as jnp
from jax import lax
from jax.experimental import pallas as pl
from jax.experimental.pallas import tpu as pltpu
from jax.sharding import PartitionSpec as P

BF = jnp.bfloat16
F32 = jnp.float32
LANES = 128
VMEM = pl.BlockSpec(memory_space=pltpu.VMEM)
SMEM = pl.BlockSpec(memory_space=pltpu.SMEM)
PARAMS = pltpu.CompilerParams(vmem_limit_bytes=14 * 1024 * 1024)


def call(body, outs, *args, smem=(), flops=1000):
    return pl.pallas_call(
        body,
        out_shape=outs,
        in_specs=[SMEM if i in smem else VMEM for i in range(len(args))],
        out_specs=[VMEM] * len(outs),
        compiler_params=PARAMS,
        cost_estimate=pl.CostEstimate(flops=flops, bytes_accessed=1000, transcendentals=0),
    )(*args)


def sds(shape, dtype):
    return jax.ShapeDtypeStruct(shape, dtype)


def onehot(row, count, base=0):
    sub = lax.broadcasted_iota(jnp.int32, (count, row.shape[1]), 0) + base
    return (sub == row).astype(F32).astype(BF)


def dot(a, b):
    return jnp.dot(a, b, preferred_element_type=F32)


def dot_t(a, b):
    return lax.dot_general(a, b, (((1,), (1,)), ((), ())), preferred_element_type=F32)


def dot_c(a, b):
    return lax.dot_general(a, b, (((0,), (0,)), ((), ())), preferred_element_type=F32)


def masks_body(owners, *outs):
    group, member = lax.axis_index("group"), lax.axis_index("member")
    per_step = len(outs) // owners.shape[0]
    for step in range(owners.shape[0]):
        root = owners[step, group]
        differ = root ^ member
        for index in range(per_step - 1):
            bit = (differ >> index) & 1
            outs[step * per_step + index][...] = jnp.full(outs[0].shape, bit, jnp.int32)
        outs[(step + 1) * per_step - 1][...] = jnp.full(outs[0].shape, (root == member).astype(jnp.int32))


def prepare_body(step, rel_ids, neg_ids, relation, rel, counts):
    hot = onehot(rel_ids[step : step + 1, :], relation.shape[1])
    rel[...] = dot(relation[...], hot).astype(BF)
    negs = neg_ids[step : step + 1, :]
    sub = lax.broadcasted_iota(jnp.int32, (counts.shape[0], negs.shape[1]), 0)
    counts[...] = jnp.sum((sub == negs).astype(F32), 1, keepdims=True)


def place(step, groups, count, rows, dest_groups, dest_rows, first=0):
    near = dest_groups[step] ^ lax.axis_index("group")
    return onehot(near * rows + dest_rows[step : step + 1, :], count * rows, first * rows)


def dest_body(step, groups, dest_groups, dest_rows, table, *refs):
    shards, dest = refs[:-1], refs[-1]
    hot = place(step, groups, groups - 1, table.shape[1], dest_groups, dest_rows)
    whole = jnp.concatenate([x[...] for x in (table, *shards)], 1)
    dest[...] = dot(whole, hot).astype(BF)


def far_body(step, groups, dest_groups, dest_rows, near, first, second, dest):
    rows, at = first.shape[1], first.shape[0]
    hot = place(step, groups, 1, rows, dest_groups, dest_rows, groups - 1)
    dest[:at, :] = near[:at, :] + dot(first[...], hot).astype(BF)
    dest[at:, :] = near[at:, :] + dot(second[...], hot).astype(BF)


def source_body(
    step, src, real, imag, rel, table, counts, dest, query, out_r, out_i, coef_pos, coef_neg
):
    rows, half = table.shape[1], real.shape[0]
    back = onehot(src[step : step + 1, :], rows)
    sr, si = dot(real[...], back), dot(imag[...], back)
    rr, ri = rel[:half, :].astype(F32), rel[half:, :].astype(F32)
    query[:half, :] = (sr * rr - si * ri).astype(BF)
    query[half:, :] = (sr * ri + si * rr).astype(BF)
    scores = dot_c(table[...], query[...])
    count = counts[...]
    scores = jnp.where(count > 0.0, scores, -jnp.inf)
    dr, di = dest[:half, :].astype(F32), dest[half:, :].astype(F32)
    qr, qi = query[:half, :].astype(F32), query[half:, :].astype(F32)
    positive = jnp.sum(qr * dr + qi * di, 0, keepdims=True)
    top = jnp.maximum(jnp.max(scores, 0, keepdims=True), positive)
    pos_exp = jnp.exp(positive - top)
    neg_exp = count * jnp.exp(scores - top)
    total = pos_exp + jnp.sum(neg_exp, 0, keepdims=True)
    pos = pos_exp / total - 1.0
    neg = (neg_exp * (1.0 / total)).astype(BF)
    coef_pos[...] = pos
    coef_neg[...] = neg
    gr = pos * dr + dot(table[:half, :], neg)
    gi = pos * di + dot(table[half:, :], neg)
    out_r[...] = dot_t((gr * rr + gi * ri).astype(BF), back).astype(BF)
    out_i[...] = dot_t((gi * rr - gr * ri).astype(BF), back).astype(BF)


def spread_body(step, groups, dest_groups, dest_rows, query, coef_pos, coef_neg, base_grad, *sends):
    rows, half = base_grad.shape[1], base_grad.shape[0] // 2
    hot = place(step, groups, groups, rows, dest_groups, dest_rows)
    for part in (0, 1):
        span = slice(part * half, (part + 1) * half)
        q = query[span, :]
        spread = dot_t((coef_pos[...] * q.astype(F32)).astype(BF), hot)
        base_grad[span, :] = spread[:, :rows] + dot_t(q, coef_neg[...])
        for k in range(1, groups):
            sends[2 * k - 2 + part][...] = spread[:, k * rows : (k + 1) * rows].astype(BF)


def merge_body(halves, base_grad, *refs):
    half = base_grad.shape[0] // 2
    for part in (0, 1):
        span = slice(part * half, (part + 1) * half)
        grad = base_grad[span, :]
        for piece, held in zip(refs[:-1], halves):
            if held is None:
                grad = grad + piece[span, :].astype(F32)
            elif held == part:
                grad = grad + piece[...].astype(F32)
        refs[-1][span, :] = grad


def update_body(table, state, merged, src_r, src_i, new_table, new_state):
    width, half = table.shape[0], src_r.shape[0]
    grads = []
    for part, source in enumerate((src_r, src_i)):
        grads.append(merged[part * half : (part + 1) * half, :] + source[...].astype(F32))
    square = sum(jnp.sum(g * g, 0, keepdims=True) for g in grads)
    after = state[...] + square * (1.0 / width)
    new_state[...] = after
    rate = lax.rsqrt(after)
    for part, grad in enumerate(grads):
        span = slice(part * half, (part + 1) * half)
        new_table[span, :] = (table[span, :].astype(F32) - grad * rate).astype(BF)


def add(a, b):
    return (a.astype(F32) + b.astype(F32)).astype(BF)


def shift(value, axis, bit):
    size = lax.axis_size(axis)
    return lax.ppermute(value, axis, [(i, i ^ bit) for i in range(size)])


def z_bits():
    bits = []
    bit = 2
    while bit < lax.axis_size("member"):
        bits.append(bit)
        bit *= 2
    return bits


def after(value, *others):
    return lax.optimization_barrier((value, *others))[0]


def gather_shards(table):
    groups, width = lax.axis_size("group"), table.shape[0]
    near = [shift(table, "group", k) for k in range(1, groups - 1)]
    if groups != 4:
        far = shift(table, "group", groups - 1)
        return near + [far[: width // 2], far[width // 2 :]]
    at = width * 3 // 5 // 16 * 16
    return near + [shift(near[0][:at], "group", 2), shift(near[1][at:], "group", 1)]


def spread_grads(sends):
    groups = lax.axis_size("group")
    if groups != 4:
        parts = [(p, shift(sends[2 * k - 2 + p], "group", k)) for k in range(1, groups) for p in (0, 1)]
        return [x for _, x in parts[:2]], lambda *earlier: parts
    xr, xi, yr, yi, dr, di = sends
    x, y = shift(dr, "group", 1), shift(di, "group", 2)
    real, imag = shift(xr, "group", 1), shift(yi, "group", 2)

    def rest(*earlier):
        y_real = shift(add(after(yr, *earlier), x), "group", 2)
        x_imag = shift(add(after(xi, *earlier), y), "group", 1)
        return [(0, y_real), (1, x_imag), (0, real), (1, imag)]

    return [x, y], rest


def per_device(
    entity,
    adagrad_state,
    relation,
    source_ids,
    relation_ids,
    dest_groups,
    dest_rows,
    negative_ids,
    owners,
):
    groups = lax.axis_size("group")
    first = lax.axis_index("member") % 2 == 0
    steps, edges = source_ids.shape
    rows, width = entity.shape
    half = width // 2
    table = entity.T
    state = adagrad_state[None, :]
    rel_t = relation.T
    dest_groups = jnp.transpose(dest_groups, (0, 2, 1))
    bits = z_bits()
    kinds = 2 + len(bits)

    def root_masks(owners):
        return call(masks_body, [sds((1, rows), jnp.int32)] * (steps * kinds), owners, smem=(0,))

    def prepare(step, earlier):
        return call(
            functools.partial(prepare_body, step),
            [sds((width, edges), BF), sds((rows, 1), F32)],
            relation_ids, negative_ids, after(rel_t, earlier),
        )

    for step in range(steps):
        real, imag = table[:half], table[half:]
        keep, give = jnp.where(first, real, imag), jnp.where(first, imag, real)
        if step == 0:
            keep, give = lax.optimization_barrier((keep, give))
            masks = root_masks(after(owners, give))
        mask = [x != 0 for x in masks[step * kinds : (step + 1) * kinds]]
        shards = gather_shards(table)
        held = jnp.where(mask[0], shift(give, "member", 1), keep)
        for turn, bit in enumerate(bits):
            held = jnp.where(mask[bit.bit_length() - 1], shift(held, "member", bit), held)
        (near,) = call(
            functools.partial(dest_body, step, groups),
            [sds((width, edges), BF)],
            dest_groups, dest_rows, table, *shards[:-2],
        )
        other = shift(after(held, near), "member", 1)
        block = jnp.where(first, held, other), jnp.where(first, other, held)
        if step == 0:
            rel, counts = prepare(0, shards[0])
        (dest,) = call(
            functools.partial(far_body, step, groups),
            [sds((width, edges), BF)],
            dest_groups, dest_rows, near, *shards[-2:],
            flops=8 * 10**9,
        )
        query, out_r, out_i, coef_pos, coef_neg = call(
            functools.partial(source_body, step),
            [sds((width, edges), BF)]
            + [sds((half, rows), BF)] * 2
            + [sds((1, edges), F32), sds((rows, edges), BF)],
            source_ids, *block, rel, table, counts, dest,
        )
        give = shift(jnp.where(first, out_i, out_r), "member", 1)
        base_grad, *sends = call(
            functools.partial(spread_body, step, groups),
            [sds((width, rows), F32)] + [sds((half, rows), BF)] * (2 * groups - 2),
            dest_groups, dest_rows, query, coef_pos, coef_neg,
        )
        early, rest = spread_grads(sends)
        part = add(jnp.where(first, out_r, out_i), give)
        for turn, bit in enumerate(bits):
            part = add(part, shift(part, "member", bit))
            if turn == 0:
                parts = rest(part)
                if step + 1 < steps:
                    ahead = prepare(step + 1, part)
        if step + 1 < steps:
            part = after(part, *ahead)
        other = shift(part, "member", 1)
        source = [jnp.where(mask[-1] & first, part, jnp.where(mask[-1], other, 0))]
        source += [jnp.where(mask[-1] & first, other, jnp.where(mask[-1], part, 0))]
        (merged,) = call(
            functools.partial(merge_body, [at for at, _ in parts]),
            [sds((width, rows), F32)],
            base_grad, *[x for _, x in parts],
            flops=8 * 10**9,
        )
        table, state = call(
            update_body, [sds((width, rows), BF), sds((1, rows), F32)], table, state, merged, *source
        )
        if step + 1 < steps:
            rel, counts = ahead
    return (table.T, state[0])


def solution(mesh):
    placed = (
        P(("group", "member"), None),
        P(("group", "member")),
        P(),
        P(None, ("group", "member")),
        P(None, ("group", "member")),
        P(None, ("group", "member"), None),
        P(None, ("group", "member")),
        P(None, ("group", "member")),
        P(),
    )
    return jax.shard_map(
        per_device,
        mesh=mesh,
        in_specs=placed,
        out_specs=(P(("group", "member"), None), P(("group", "member"))),
        check_vma=False,
    )
```
